32 devices in a mesh: expert: 4 (over x, core), fsdp: 8 (over z, y).
Axes of the slice: x: 2, y: 2, z: 4, core: 2. Of those that a mesh axis runs over, the one named last changes fastest.
Arguments:
- tokens: bfloat16 [4096, 2048], P(('expert', 'fsdp')), may hold values from -6 to 6
- expert_ids: int32 [4096, 1], P(('expert', 'fsdp')), may hold values from 0 to 7; in each aligned block of 128 rows (0 to 127, 128 to 255, ...) at most 24 rows name the same one
- gate_weight: bfloat16 [8, 2048, 8192], P('expert', None, 'fsdp'), may hold values from -0.125 to 0.125
- up_weight: bfloat16 [8, 2048, 8192], P('expert', None, 'fsdp'), may hold values from -0.125 to 0.125
- hidden_grad: bfloat16 [8, 768, 8192], P('expert', None, 'fsdp'), may hold values from -0.1796875 to 0.1796875
Outputs:
- hidden: bfloat16 [8, 768, 8192], P('expert', None, 'fsdp')
- gate_grad: float32 [8, 2048, 8192], P('expert', None, 'fsdp')
- up_grad: float32 [8, 2048, 8192], P('expert', None, 'fsdp')
The draws below stay inside these ranges and needn't reach their ends.
Inputs may be any that keep to these rules, and one draw needn't show every extreme that they name: `expert_ids`: within the tokens of one device (aligned blocks of 128 rows) no expert is named more than 24 times, a bound that some block reaches.
All inputs are finite; a program needn't handle non-finite values.
Results may differ from the reference program's by a relative error of at most 0.003.
Values may be sent and summed in bfloat16 or wider, within the bound.
A program may use at most 192 MiB of HBM per device.

```python
import math
import jax
import jax.numpy as jnp
import numpy as np
from jax import lax

D = 2048
FF = 8192
TOK_DEV = 128
EXPERTS = 8
CAP = 24
TOKENS = 4096
SLOTS = 768
N_EXPERT = 4
N_FSDP = 8


def block_scale(stream_key, dims, shards, least, top_value):
    def one(position, blocks):
        draws = jax.random.uniform(jax.random.fold_in(jax.random.fold_in(stream_key, 6), position), (blocks,), jnp.float32, least / len(shards), top_value / len(shards))
        return jnp.repeat(jnp.exp(draws), dims[position] // blocks).reshape((-1,) + (1,) * (len(dims) - position - 1))

    level = one(*shards[0])
    for cut in shards[1:]:
        level = level * one(*cut)
    return level


def deal_out(own_key, own, number, rows, number_of, top, reach, skew):
    order = jax.random.permutation(own_key, number_of)
    packed, ordinary = shares(number_of, rows * top, reach, skew, True), shares(number_of, rows * top, reach, skew, False)
    places = jnp.arange(number_of)

    def named(tallies, rotation):
        used = int((tallies > 0).sum())
        fixed = max(1, used // 4)
        passed = fixed + (places - fixed + rotation * (used - fixed)) % max(1, number_of - fixed)
        return jnp.zeros((number_of,), jnp.int32).at[order[jnp.where(places < fixed, places, passed)]].set(jnp.asarray(tallies, jnp.int32))

    tallies = jnp.where(number % 4 == 0, named(packed, number // 4), named(ordinary, number - number // 4 - 1))
    mixed = jax.random.permutation(jax.random.fold_in(own, 3), number_of)
    donor, sink = mixed[0:number_of // 2 * 2:2], mixed[1:number_of // 2 * 2:2]
    room = jnp.minimum(tallies[donor] - 1, reach - tallies[sink]) // 2
    room = jnp.where((donor == order[0]) | (sink == order[0]) | (tallies[sink] == 0), 0, jnp.maximum(room, 0))
    passed = jax.random.randint(jax.random.fold_in(own, 4), (number_of // 2,), 0, 1 << 20) % (room + 1)
    tallies = tallies.at[donor].add(-passed).at[sink].add(passed)
    members = jnp.searchsorted(jnp.cumsum(tallies), jnp.arange(rows * top), side="right").astype(jnp.int32)
    grid = members.reshape(top, rows).T
    grid = grid[jax.random.permutation(jax.random.fold_in(own, 1), rows)]
    rotation = jax.random.randint(jax.random.fold_in(own, 2), (rows, 1), 0, top)
    return jnp.take_along_axis(grid, (jnp.arange(top)[None, :] + rotation) % top, axis=1)


def shares(count, total, bound, skew, full):
    loads = [(1 << 20) // math.isqrt(grade ** skew) + 1 for grade in range(1, count + 1)]
    largest = bound if full else min(bound, max(-(-total // count), total * loads[0] // sum(loads)))
    least = 1 if total - largest >= count - 1 else 0
    given, spare = [largest] + [least] * (count - 1), total - largest - least * (count - 1)
    while spare > 0:
        free = [i for i in range(1, count) if given[i] < largest] or [i for i in range(1, count) if given[i] < bound]
        whole, budget = sum([loads[i] for i in free]), spare
        for i in free:
            addition = min(bound - given[i], max(1, budget * loads[i] // whole), spare)
            given[i] = given[i] + addition
            spare = spare - addition
    return np.array(given)


def bell_draw(rng, dims, spread, bound, split=(), kind=jnp.bfloat16):
    gain = block_scale(rng, dims, split, -0.22, 0.18) if split else 1.0
    entries = jax.random.normal(rng, dims, jnp.float32) * spread * gain
    return jnp.minimum(jnp.maximum(entries, -bound), bound).astype(kind)


def setup_inputs(seed: int = 0) -> dict:
    seeds = jax.random.split(jax.random.key(seed), 6)
    tokens = bell_draw(seeds[0], (TOKENS, D), 1.0, 6.0, ((0, 32),))
    expert_ids_keys = jax.random.split(jax.random.fold_in(seeds[1], 1), TOKENS // TOK_DEV)
    expert_ids_turns = jax.random.permutation(jax.random.fold_in(seeds[1], 3), TOKENS // TOK_DEV)
    expert_ids = jax.vmap(lambda own, number: deal_out(jax.random.fold_in(seeds[1], 2), own, number, TOK_DEV, EXPERTS, 1, CAP, 2))(expert_ids_keys, expert_ids_turns).reshape((TOKENS, 1))
    gate_weight = bell_draw(seeds[2], (EXPERTS, D, FF), D ** -0.5, 0.125, ((0, 4), (2, 8)))
    up_weight = bell_draw(seeds[3], (EXPERTS, D, FF), D ** -0.5, 0.125, ((0, 4), (2, 8)))
    hidden_grad = bell_draw(seeds[4], (EXPERTS, SLOTS, FF), 0.03, 0.1796875, ((0, 4), (2, 8)))
    return {"tokens": tokens, "expert_ids": expert_ids, "gate_weight": gate_weight, "up_weight": up_weight, "hidden_grad": hidden_grad}


def expert_pass(args):
    rows, gate_w, up_w, cotan = args
    gate = jnp.dot(rows, gate_w, preferred_element_type=jnp.float32)
    upval = jnp.dot(rows, up_w, preferred_element_type=jnp.float32)
    sigma = 1.0 / (1.0 + jnp.exp(-gate))
    active = gate * sigma
    hidden = (active * upval).astype(jnp.bfloat16)
    cot = cotan.astype(jnp.float32)
    gate_delta = (cot * upval * sigma * (1.0 + gate * (1.0 - sigma))).astype(jnp.bfloat16)
    up_delta = (cot * active).astype(jnp.bfloat16)
    gate_grad = jnp.dot(rows.T, gate_delta, preferred_element_type=jnp.float32)
    up_grad = jnp.dot(rows.T, up_delta, preferred_element_type=jnp.float32)
    return hidden, gate_grad, up_grad


def reference(tokens, expert_ids, gate_weight, up_weight, hidden_grad):
    route = expert_ids[:, 0].astype(jnp.int32)
    blocks = N_EXPERT * N_FSDP
    grouped = route.reshape(blocks, TOK_DEV)
    onehot = (grouped[:, :, None] == jnp.arange(EXPERTS, dtype=jnp.int32)[None, None, :]).astype(jnp.int32)
    before = jnp.cumsum(onehot, axis=1) - onehot
    rank = jnp.sum(before * onehot, axis=2).astype(jnp.int32)
    slot = (jnp.arange(blocks, dtype=jnp.int32)[:, None] * CAP + rank).reshape(-1).astype(jnp.int32)
    dispatched = jnp.zeros((EXPERTS, SLOTS, D), jnp.bfloat16).at[route, slot].set(tokens)
    hidden, gate_grad, up_grad = lax.map(expert_pass, (dispatched, gate_weight, up_weight, hidden_grad))
    return hidden, gate_grad, up_grad
```

```python
import functools

import jax
import jax.numpy as jnp
from jax import lax
from jax.experimental import pallas as pl
from jax.experimental.pallas import tpu as pltpu
from jax.sharding import PartitionSpec as P

CAP = 24
MESH = pl.DeviceIdType.MESH
UP, DOWN, ACROSS = 0, 1, 2


def gather_kernel(levels, packed, rows, send_sem, first_sem, recv_sem, own_sem):
    e = lax.axis_index("expert")
    f = lax.axis_index("fsdp")
    pair, core = e // 2, e % 2
    z, y = f // 2, f % 2
    peers = [e, pair * 2 + (1 - core), (1 - pair) * 2 + core, (1 - pair) * 2 + (1 - core)]
    has_up, has_down = z < levels - 1, z > 0
    across = f + 1 - 2 * y

    barrier = pltpu.get_barrier_semaphore()

    def greet(device):
        pl.semaphore_signal(barrier, inc=1, device_id=device, device_id_type=MESH)

    for k in (1, 2, 3):
        greet((peers[k], f))
    greet((e, across))

    @pl.when(has_up)
    def _():
        greet((e, f + 2))

    @pl.when(has_down)
    def _():
        greet((e, f - 2))

    both = jnp.logical_and(has_up, has_down)

    @pl.when(both)
    def _():
        pl.semaphore_wait(barrier, 6)

    @pl.when(jnp.logical_not(both))
    def _():
        pl.semaphore_wait(barrier, 5)

    def copy(kind, fp, k, src=None):
        s = peers[k]
        target = {UP: f + 2, DOWN: f - 2, ACROSS: across}[kind]
        return pltpu.make_async_remote_copy(
            src_ref=rows.at[fp, s] if src is None else src,
            dst_ref=rows.at[fp, s],
            send_sem=send_sem.at[kind, fp, s],
            recv_sem=recv_sem.at[fp, s],
            device_id=(e, target),
            device_id_type=MESH,
        )

    def first(k):
        return pltpu.make_async_remote_copy(
            src_ref=packed.at[peers[k]],
            dst_ref=rows.at[f, e],
            send_sem=first_sem.at[k],
            recv_sem=recv_sem.at[f, e],
            device_id=(peers[k], f),
            device_id_type=MESH,
        )

    def arrived(fp, k):
        piece = rows.at[fp, peers[k]]
        pltpu.make_async_copy(piece, piece, recv_sem.at[fp, peers[k]]).wait()

    def along(fp, k, act, up=True, down=True, src=None):
        if up:

            @pl.when(has_up)
            def _():
                act(copy(UP, fp, k, src))

        if down:

            @pl.when(has_down)
            def _():
                act(copy(DOWN, fp, k, src))

    def start(c):
        c.start()

    def sent(c):
        c.wait_send()

    own = pltpu.make_async_copy(packed.at[e], rows.at[f, e], own_sem)
    own.start()
    for k in (2, 3, 1):
        first(k).start()
    copy(ACROSS, f, 0, packed.at[e]).start()
    along(f, 0, start, src=packed.at[e])
    for k in (1, 2, 3):
        arrived(f, k)
        along(f, k, start)
        copy(ACROSS, f, k).start()
    arrived(across, 0)
    along(across, 0, start)
    for d in range(1, levels):
        for k in (0, 1, 2, 3):

            @pl.when(z >= d)
            def _():
                fp = f - 2 * d
                arrived(fp, k)
                along(fp, k, start, down=False)
                if k > 0:
                    copy(ACROSS, fp, k).start()

            @pl.when(z + d < levels)
            def _():
                fp = f + 2 * d
                arrived(fp, k)
                along(fp, k, start, up=False)
                if k > 0:
                    copy(ACROSS, fp, k).start()

        @pl.when(z >= d)
        def _():
            arrived(across - 2 * d, 0)
            along(across - 2 * d, 0, start, down=False)

        @pl.when(z + d < levels)
        def _():
            arrived(across + 2 * d, 0)
            along(across + 2 * d, 0, start, up=False)

    for level in range(levels):
        for k in (1, 2, 3):
            arrived(level * 2 + 1 - y, k)

    own.wait()
    for k in (2, 3, 1):
        first(k).wait_send()
    copy(ACROSS, f, 0, packed.at[e]).wait_send()
    along(f, 0, sent, src=packed.at[e])
    for k in (1, 2, 3):
        along(f, k, sent)
        copy(ACROSS, f, k).wait_send()
    along(across, 0, sent)
    for d in range(1, levels):

        @pl.when(z >= d)
        def _():
            for k in (0, 1, 2, 3):
                along(f - 2 * d, k, sent, down=False)
                if k > 0:
                    copy(ACROSS, f - 2 * d, k).wait_send()
            along(across - 2 * d, 0, sent, down=False)

        @pl.when(z + d < levels)
        def _():
            for k in (0, 1, 2, 3):
                along(f + 2 * d, k, sent, up=False)
                if k > 0:
                    copy(ACROSS, f + 2 * d, k).wait_send()
            along(across + 2 * d, 0, sent, up=False)


def gather_rows(packed, members):
    owners, height, model = packed.shape
    return pl.pallas_call(
        functools.partial(gather_kernel, members // 2),
        out_shape=jax.ShapeDtypeStruct((members, owners, height, model), packed.dtype),
        in_specs=[pl.BlockSpec(memory_space=pl.ANY)],
        out_specs=pl.BlockSpec(memory_space=pl.ANY),
        scratch_shapes=[
            pltpu.SemaphoreType.DMA((3, members, owners)),
            pltpu.SemaphoreType.DMA((owners,)),
            pltpu.SemaphoreType.DMA((members, owners)),
            pltpu.SemaphoreType.DMA,
        ],
        compiler_params=pltpu.CompilerParams(collective_id=0, has_side_effects=True),
    )(packed)


def fold(rows, gate_part, up_part, grad_part):
    gate = jnp.einsum("grd,gdf->grf", rows, gate_part, preferred_element_type=jnp.float32)
    upval = jnp.einsum("grd,gdf->grf", rows, up_part, preferred_element_type=jnp.float32)
    cotan = grad_part.astype(jnp.float32)
    sigma = 1.0 / (1.0 + jnp.exp(-gate))
    active = gate * sigma
    hidden = (active * upval).astype(jnp.bfloat16)
    gate_delta = (cotan * upval * sigma * (1.0 + gate * (1.0 - sigma))).astype(jnp.bfloat16)
    up_delta = (cotan * active).astype(jnp.bfloat16)
    gate_sum = jnp.einsum("grd,grf->gdf", rows, gate_delta, preferred_element_type=jnp.float32)
    up_sum = jnp.einsum("grd,grf->gdf", rows, up_delta, preferred_element_type=jnp.float32)
    return hidden, gate_sum, up_sum


def on_device(tokens, expert_ids, gate_weight, up_weight, hidden_grad):
    owners = lax.axis_size("expert")
    members = lax.axis_size("fsdp")
    per_owner, model = gate_weight.shape[:2]
    route = expert_ids[:, 0]
    total_experts = per_owner * owners
    onehot = (route[:, None] == jnp.arange(total_experts, dtype=jnp.int32)[None, :]).astype(
        jnp.int32
    )
    rank = jnp.sum((jnp.cumsum(onehot, axis=0) - onehot) * onehot, axis=1)
    target = route * CAP + rank
    placing = (
        jnp.arange(total_experts * CAP, dtype=jnp.int32)[:, None] == target[None, :]
    ).astype(jnp.bfloat16)
    packed = jnp.dot(placing, tokens, preferred_element_type=jnp.float32).astype(jnp.bfloat16)
    rows = gather_rows(packed.reshape(owners, per_owner * CAP, model), members)
    rows = rows.reshape(members, owners, per_owner, CAP, model).transpose(2, 1, 0, 3, 4)
    rows = rows.reshape(per_owner, owners * members * CAP, model)
    return fold(rows, gate_weight, up_weight, hidden_grad)


def solution(mesh):
    in_specs = (
        P(("expert", "fsdp"), None),
        P(("expert", "fsdp"), None),
        P("expert", None, "fsdp"),
        P("expert", None, "fsdp"),
        P("expert", None, "fsdp"),
    )
    out_specs = (P("expert", None, "fsdp"), P("expert", None, "fsdp"), P("expert", None, "fsdp"))
    return jax.shard_map(
        on_device, mesh=mesh, in_specs=in_specs, out_specs=out_specs, check_vma=False
    )
```

```python
import functools

import jax
import jax.numpy as jnp
from jax import lax
from jax.experimental import pallas as pl
from jax.experimental.pallas import tpu as pltpu
from jax.sharding import PartitionSpec as P

CAP = 24
MESH = pl.DeviceIdType.MESH
UP, DOWN, ACROSS = 0, 1, 2


def gather_kernel(
    levels,
    tile,
    packed,
    gate_hbm,
    up_hbm,
    cotan_hbm,
    rows,
    slots_out,
    hidden_out,
    gate_out,
    up_out,
    gate_w,
    up_w,
    raw,
    cotan,
    block,
    hidden,
    gate_delta,
    up_delta,
    send_sem,
    first_sem,
    recv_sem,
    own_sem,
    load_sem,
    store_sem,
):
    weights = [
        pltpu.make_async_copy(gate_hbm, gate_w, load_sem.at[0]),
        pltpu.make_async_copy(up_hbm, up_w, load_sem.at[1]),
    ]
    e = lax.axis_index("expert")
    f = lax.axis_index("fsdp")
    pair, core = e // 2, e % 2
    z, y = f // 2, f % 2
    peers = [e, pair * 2 + (1 - core), (1 - pair) * 2 + core, (1 - pair) * 2 + (1 - core)]
    has_up, has_down = z < levels - 1, z > 0
    across = f + 1 - 2 * y

    barrier = pltpu.get_barrier_semaphore()

    def greet(device):
        pl.semaphore_signal(barrier, inc=1, device_id=device, device_id_type=MESH)

    for k in (1, 2, 3):
        greet((peers[k], f))
    greet((e, across))

    @pl.when(has_up)
    def _():
        greet((e, f + 2))

    @pl.when(has_down)
    def _():
        greet((e, f - 2))

    both = jnp.logical_and(has_up, has_down)

    @pl.when(both)
    def _():
        pl.semaphore_wait(barrier, 6)

    @pl.when(jnp.logical_not(both))
    def _():
        pl.semaphore_wait(barrier, 5)

    def copy(kind, fp, k, src=None):
        s = peers[k]
        target = {UP: f + 2, DOWN: f - 2, ACROSS: across}[kind]
        return pltpu.make_async_remote_copy(
            src_ref=rows.at[fp, s] if src is None else src,
            dst_ref=rows.at[fp, s],
            send_sem=send_sem.at[kind, fp, s],
            recv_sem=recv_sem.at[fp, s],
            device_id=(e, target),
            device_id_type=MESH,
        )

    def first(k):
        return pltpu.make_async_remote_copy(
            src_ref=packed.at[peers[k]],
            dst_ref=rows.at[f, e],
            send_sem=first_sem.at[k],
            recv_sem=recv_sem.at[f, e],
            device_id=(peers[k], f),
            device_id_type=MESH,
        )

    def arrived(fp, k):
        piece = rows.at[fp, peers[k]]
        pltpu.make_async_copy(piece, piece, recv_sem.at[fp, peers[k]]).wait()

    def along(fp, k, act, up=True, down=True, src=None):
        if up:

            @pl.when(has_up)
            def _():
                act(copy(UP, fp, k, src))

        if down:

            @pl.when(has_down)
            def _():
                act(copy(DOWN, fp, k, src))

    def start(c):
        c.start()

    def sent(c):
        c.wait_send()

    groups, owners, height, model = block.shape
    width = gate_w.shape[2]

    def stores(level):
        places = pl.ds(pl.multiple_of(level * height, 16), height)
        return [
            pltpu.make_async_copy(v, h.at[:, :, places], store_sem.at[i])
            for i, (v, h) in enumerate(
                (
                    (block, slots_out),
                    (hidden, hidden_out),
                    (gate_delta, gate_out),
                    (up_delta, up_out),
                )
            )
        ]

    def fetch(level):
        for k in (1, 2, 3):
            arrived(level * 2 + 1 - y, k)
        places = pl.ds(pl.multiple_of(level * height, 16), height)
        loads = [
            pltpu.make_async_copy(rows.at[pl.ds(level * 2, 2)], raw, load_sem.at[2]),
            pltpu.make_async_copy(cotan_hbm.at[:, :, places], cotan, load_sem.at[3]),
        ]
        for c in loads:
            c.start()
        for c in loads:
            c.wait()
        for s in range(owners):
            for n in range(0, model, 512):
                low = raw[0, s, :, n : n + 512].astype(jnp.float32)
                high = raw[1, s, :, n : n + 512].astype(jnp.float32)
                for g in range(groups):
                    part = slice(g * CAP, (g + 1) * CAP)
                    both_parts = jnp.concatenate([low[part], high[part]], axis=0)
                    block[g, s, :, n : n + 512] = both_parts.astype(block.dtype)

    def multiply(level, g):
        flat = block[g].reshape(owners * height, model)

        @pl.loop(0, width // tile)
        def _(n):
            cols = pl.ds(pl.multiple_of(n * tile, tile), tile)
            gate = jnp.dot(flat, gate_w[g, :, cols], preferred_element_type=jnp.float32)
            upval = jnp.dot(flat, up_w[g, :, cols], preferred_element_type=jnp.float32)
            cot = cotan[g, :, :, cols].reshape(owners * height, tile).astype(jnp.float32)
            sigma = 1.0 / (1.0 + jnp.exp(-gate))
            active = gate * sigma
            slope = sigma * (1.0 + gate * (1.0 - sigma))

            def put(ref, value):
                value = value.astype(ref.dtype).reshape(owners, height, tile)
                ref[g, :, :, cols] = value

            put(hidden, active * upval)
            put(gate_delta, cot * upval * slope)
            put(up_delta, cot * active)

    def flush(level):
        for c in stores(level):
            c.start()
        for c in stores(level):
            c.wait()

    own = pltpu.make_async_copy(packed.at[e], rows.at[f, e], own_sem)
    own.start()
    for k in (2, 3, 1):
        first(k).start()
    copy(ACROSS, f, 0, packed.at[e]).start()
    along(f, 0, start, src=packed.at[e])
    for c in weights:
        c.start()
    for k in (1, 2, 3):
        arrived(f, k)
        along(f, k, start)
        copy(ACROSS, f, k).start()
    arrived(across, 0)
    along(across, 0, start)
    own.wait()
    for c in weights:
        c.wait()

    def pass_on(d, k):
        @pl.when(z >= d)
        def _():
            arrived(f - 2 * d, k)
            along(f - 2 * d, k, start, down=False)
            if k > 0:
                copy(ACROSS, f - 2 * d, k).start()

        @pl.when(z + d < levels)
        def _():
            arrived(f + 2 * d, k)
            along(f + 2 * d, k, start, up=False)
            if k > 0:
                copy(ACROSS, f + 2 * d, k).start()

    def pass_across(d):
        @pl.when(z >= d)
        def _():
            arrived(across - 2 * d, 0)
            along(across - 2 * d, 0, start, down=False)

        @pl.when(z + d < levels)
        def _():
            arrived(across + 2 * d, 0)
            along(across + 2 * d, 0, start, up=False)

    def work(d, between):
        below, above = z >= d, z + d < levels
        nearer = z + d - 2 * d * ((z - d + levels) // levels)
        paired = jnp.logical_and(jnp.logical_and(below, above), d > 0)
        for level, valid in ((nearer, jnp.logical_or(below, above)), (z + d, paired)):

            @pl.when(valid)
            def _():
                fetch(level)

            between()
            for g in range(groups):

                @pl.when(valid)
                def _():
                    multiply(level, g)

                between()

            @pl.when(valid)
            def _():
                flush(level)

    @pl.loop(1, levels + 1)
    def _(d):
        pending = [functools.partial(pass_on, d, k) for k in range(4)]
        pending.append(functools.partial(pass_across, d))

        def between():
            if pending:
                pending.pop(0)()

        between()
        between()
        work(d - 1, between)

    for k in (2, 3, 1):
        first(k).wait_send()
    copy(ACROSS, f, 0, packed.at[e]).wait_send()
    along(f, 0, sent, src=packed.at[e])
    for k in (1, 2, 3):
        along(f, k, sent)
        copy(ACROSS, f, k).wait_send()
    along(across, 0, sent)
    for d in range(1, levels):

        @pl.when(z >= d)
        def _():
            for k in (0, 1, 2, 3):
                along(f - 2 * d, k, sent, down=False)
                if k > 0:
                    copy(ACROSS, f - 2 * d, k).wait_send()
            along(across - 2 * d, 0, sent, down=False)

        @pl.when(z + d < levels)
        def _():
            for k in (0, 1, 2, 3):
                along(f + 2 * d, k, sent, up=False)
                if k > 0:
                    copy(ACROSS, f + 2 * d, k).wait_send()
            along(across + 2 * d, 0, sent, up=False)


def gather_rows(packed, gate_part, up_part, grad_part, members):
    owners, height, model = packed.shape
    groups, _, width = gate_part.shape
    dtype = packed.dtype
    spread = (groups, owners, members * CAP)
    narrow = jax.ShapeDtypeStruct(spread + (width,), dtype)
    pair = (groups, owners, 2 * CAP)
    return pl.pallas_call(
        functools.partial(gather_kernel, members // 2, min(256, width)),
        out_shape=(
            jax.ShapeDtypeStruct((members, owners, height, model), dtype),
            jax.ShapeDtypeStruct(spread + (model,), dtype),
            narrow,
            narrow,
            narrow,
        ),
        in_specs=[pl.BlockSpec(memory_space=pl.ANY)] * 4,
        out_specs=(pl.BlockSpec(memory_space=pl.ANY),) * 5,
        scratch_shapes=[
            pltpu.VMEM((groups, model, width), dtype),
            pltpu.VMEM((groups, model, width), dtype),
            pltpu.VMEM((2, owners, height, model), dtype),
            pltpu.VMEM(pair + (width,), dtype),
            pltpu.VMEM(pair + (model,), dtype),
            pltpu.VMEM(pair + (width,), dtype),
            pltpu.VMEM(pair + (width,), dtype),
            pltpu.VMEM(pair + (width,), dtype),
            pltpu.SemaphoreType.DMA((3, members, owners)),
            pltpu.SemaphoreType.DMA((owners,)),
            pltpu.SemaphoreType.DMA((members, owners)),
            pltpu.SemaphoreType.DMA,
            pltpu.SemaphoreType.DMA((4,)),
            pltpu.SemaphoreType.DMA((4,)),
        ],
        compiler_params=pltpu.CompilerParams(
            collective_id=0, has_side_effects=True, vmem_limit_bytes=48 * 1024 * 1024
        ),
    )(packed, gate_part, up_part, grad_part.reshape(spread + (width,)))


def grad_kernel(rows_ref, gate_ref, up_ref, gate_out, up_out):
    dims = (((0,), (0,)), ((), ()))
    rows = rows_ref[...]
    gate_out[...] = lax.dot_general(rows, gate_ref[...], dims, preferred_element_type=jnp.float32)
    up_out[...] = lax.dot_general(rows, up_ref[...], dims, preferred_element_type=jnp.float32)


def weight_grads(rows, gate_delta, up_delta):
    groups, slots, model = rows.shape
    width = gate_delta.shape[2]
    tile, cut = min(512, model), min(1024, width)
    delta = pl.BlockSpec((None, slots, cut), lambda g, n, m: (g, 0, n))
    out = pl.BlockSpec((None, tile, cut), lambda g, n, m: (g, m, n))
    shape = jax.ShapeDtypeStruct((groups, model, width), jnp.float32)
    return pl.pallas_call(
        grad_kernel,
        grid=(groups, width // cut, model // tile),
        out_shape=(shape, shape),
        in_specs=[pl.BlockSpec((None, slots, tile), lambda g, n, m: (g, 0, m)), delta, delta],
        out_specs=(out, out),
        compiler_params=pltpu.CompilerParams(vmem_limit_bytes=48 * 1024 * 1024),
        cost_estimate=pl.CostEstimate(
            flops=4 * groups * slots * model * width,
            bytes_accessed=2 * groups * slots * (model + 2 * width) + 8 * groups * model * width,
            transcendentals=0,
        ),
    )(rows, gate_delta, up_delta)


def on_device(tokens, expert_ids, gate_weight, up_weight, hidden_grad):
    owners = lax.axis_size("expert")
    members = lax.axis_size("fsdp")
    per_owner, model = gate_weight.shape[:2]
    route = expert_ids[:, 0]
    total_experts = per_owner * owners
    onehot = (route[:, None] == jnp.arange(total_experts, dtype=jnp.int32)[None, :]).astype(
        jnp.int32
    )
    rank = jnp.sum((jnp.cumsum(onehot, axis=0) - onehot) * onehot, axis=1)
    target = route * CAP + rank
    placing = (
        jnp.arange(total_experts * CAP, dtype=jnp.int32)[:, None] == target[None, :]
    ).astype(jnp.bfloat16)
    packed = jnp.dot(placing, tokens, preferred_element_type=jnp.float32).astype(jnp.bfloat16)
    blocks = packed.reshape(owners, per_owner * CAP, model)
    _, rows, hidden, gate_delta, up_delta = gather_rows(
        blocks, gate_weight, up_weight, hidden_grad, members
    )

    def by_slot(x):
        return x.reshape(per_owner, owners * members * CAP, x.shape[3])

    gate_sum, up_sum = weight_grads(by_slot(rows), by_slot(gate_delta), by_slot(up_delta))
    return by_slot(hidden), gate_sum, up_sum


def solution(mesh):
    in_specs = (
        P(("expert", "fsdp"), None),
        P(("expert", "fsdp"), None),
        P("expert", None, "fsdp"),
        P("expert", None, "fsdp"),
        P("expert", None, "fsdp"),
    )
    out_specs = (P("expert", None, "fsdp"), P("expert", None, "fsdp"), P("expert", None, "fsdp"))
    return jax.shard_map(
        on_device, mesh=mesh, in_specs=in_specs, out_specs=out_specs, check_vma=False
    )
```

```python
import functools

import jax
import jax.numpy as jnp
from jax import lax
from jax.experimental import pallas as pl
from jax.experimental.pallas import tpu as pltpu
from jax.sharding import PartitionSpec as P

CAP = 24
MESH = pl.DeviceIdType.MESH
UP, DOWN, ACROSS = 0, 1, 2


def gather_kernel(
    levels,
    tile,
    packed,
    gate_hbm,
    up_hbm,
    cotan_hbm,
    rows,
    slots_out,
    hidden_out,
    gate_out,
    up_out,
    gate_w,
    up_w,
    raw,
    cotan,
    block,
    hidden,
    gate_delta,
    up_delta,
    send_sem,
    first_sem,
    recv_sem,
    own_sem,
    load_sem,
    store_sem,
):
    weights = [
        pltpu.make_async_copy(gate_hbm, gate_w, load_sem.at[0]),
        pltpu.make_async_copy(up_hbm, up_w, load_sem.at[1]),
    ]
    e = lax.axis_index("expert")
    f = lax.axis_index("fsdp")
    pair, core = e // 2, e % 2
    z, y = f // 2, f % 2
    peers = [e, pair * 2 + (1 - core), (1 - pair) * 2 + core, (1 - pair) * 2 + (1 - core)]
    has_up, has_down = z < levels - 1, z > 0
    across = f + 1 - 2 * y

    barrier = pltpu.get_barrier_semaphore()

    def greet(device):
        pl.semaphore_signal(barrier, inc=1, device_id=device, device_id_type=MESH)

    for k in (1, 2, 3):
        greet((peers[k], f))
    greet((e, across))

    @pl.when(has_up)
    def _():
        greet((e, f + 2))

    @pl.when(has_down)
    def _():
        greet((e, f - 2))

    both = jnp.logical_and(has_up, has_down)

    @pl.when(both)
    def _():
        pl.semaphore_wait(barrier, 6)

    @pl.when(jnp.logical_not(both))
    def _():
        pl.semaphore_wait(barrier, 5)

    def copy(kind, fp, k, src=None):
        s = peers[k]
        target = {UP: f + 2, DOWN: f - 2, ACROSS: across}[kind]
        return pltpu.make_async_remote_copy(
            src_ref=rows.at[fp, s] if src is None else src,
            dst_ref=rows.at[fp, s],
            send_sem=send_sem.at[kind, fp, s],
            recv_sem=recv_sem.at[fp, s],
            device_id=(e, target),
            device_id_type=MESH,
        )

    def first(k):
        return pltpu.make_async_remote_copy(
            src_ref=packed.at[peers[k]],
            dst_ref=rows.at[f, e],
            send_sem=first_sem.at[k],
            recv_sem=recv_sem.at[f, e],
            device_id=(peers[k], f),
            device_id_type=MESH,
        )

    def arrived(fp, k):
        piece = rows.at[fp, peers[k]]
        pltpu.make_async_copy(piece, piece, recv_sem.at[fp, peers[k]]).wait()

    def along(fp, k, act, up=True, down=True, src=None):
        if up:

            @pl.when(has_up)
            def _():
                act(copy(UP, fp, k, src))

        if down:

            @pl.when(has_down)
            def _():
                act(copy(DOWN, fp, k, src))

    def start(c):
        c.start()

    def sent(c):
        c.wait_send()

    groups, owners, height, model = block.shape
    width = gate_w.shape[2]

    def stores(level):
        places = pl.ds(pl.multiple_of(level * height, 16), height)
        return [
            pltpu.make_async_copy(v, h.at[:, :, places], store_sem.at[i])
            for i, (v, h) in enumerate(
                (
                    (block, slots_out),
                    (hidden, hidden_out),
                    (gate_delta, gate_out),
                    (up_delta, up_out),
                )
            )
        ]

    def fetch(level):
        for k in (1, 2, 3):
            arrived(level * 2 + 1 - y, k)
        places = pl.ds(pl.multiple_of(level * height, 16), height)
        loads = [
            pltpu.make_async_copy(rows.at[pl.ds(level * 2, 2)], raw, load_sem.at[2]),
            pltpu.make_async_copy(cotan_hbm.at[:, :, places], cotan, load_sem.at[3]),
        ]
        for c in loads:
            c.start()
        for c in loads:
            c.wait()
        for s in range(owners):
            for n in range(0, model, 512):
                low = raw[0, s, :, n : n + 512].astype(jnp.float32)
                high = raw[1, s, :, n : n + 512].astype(jnp.float32)
                for g in range(groups):
                    part = slice(g * CAP, (g + 1) * CAP)
                    both_parts = jnp.concatenate([low[part], high[part]], axis=0)
                    block[g, s, :, n : n + 512] = both_parts.astype(block.dtype)

    def multiply(level, g):
        flat = block[g].reshape(owners * height, model)

        @pl.loop(0, width // tile)
        def _(n):
            cols = pl.ds(pl.multiple_of(n * tile, tile), tile)
            gate = jnp.dot(flat, gate_w[g, :, cols], preferred_element_type=jnp.float32)
            upval = jnp.dot(flat, up_w[g, :, cols], preferred_element_type=jnp.float32)
            cot = cotan[g, :, :, cols].reshape(owners * height, tile).astype(jnp.float32)
            sigma = 1.0 / (1.0 + jnp.exp(-gate))
            active = gate * sigma
            slope = sigma * (1.0 + gate * (1.0 - sigma))

            def put(ref, value):
                value = value.astype(ref.dtype).reshape(owners, height, tile)
                ref[g, :, :, cols] = value

            put(hidden, active * upval)
            put(gate_delta, cot * upval * slope)
            put(up_delta, cot * active)

    def flush(level):
        for c in stores(level):
            c.start()
        for c in stores(level):
            c.wait()

    own = pltpu.make_async_copy(packed.at[e], rows.at[f, e], own_sem)
    own.start()
    for k in (2, 3, 1):
        first(k).start()
    copy(ACROSS, f, 0, packed.at[e]).start()
    along(f, 0, start, src=packed.at[e])
    for c in weights:
        c.start()
    for k in (1, 2, 3):
        arrived(f, k)
        along(f, k, start)
        copy(ACROSS, f, k).start()
    arrived(across, 0)
    along(across, 0, start)
    own.wait()
    for c in weights:
        c.wait()

    def pass_on(d, k):
        @pl.when(z >= d)
        def _():
            arrived(f - 2 * d, k)
            along(f - 2 * d, k, start, down=False)
            if k > 0:
                copy(ACROSS, f - 2 * d, k).start()

        @pl.when(z + d < levels)
        def _():
            arrived(f + 2 * d, k)
            along(f + 2 * d, k, start, up=False)
            if k > 0:
                copy(ACROSS, f + 2 * d, k).start()

    def pass_across(d):
        @pl.when(z >= d)
        def _():
            arrived(across - 2 * d, 0)
            along(across - 2 * d, 0, start, down=False)

        @pl.when(z + d < levels)
        def _():
            arrived(across + 2 * d, 0)
            along(across + 2 * d, 0, start, up=False)

    def work(d, between):
        below, above = z >= d, z + d < levels
        nearer = z + d - 2 * d * ((z - d + levels) // levels)
        paired = jnp.logical_and(jnp.logical_and(below, above), d > 0)
        for level, valid in ((nearer, jnp.logical_or(below, above)), (z + d, paired)):

            @pl.when(valid)
            def _():
                fetch(level)

            between()
            for g in range(groups):

                @pl.when(valid)
                def _():
                    multiply(level, g)

                between()

            @pl.when(valid)
            def _():
                flush(level)

    @pl.loop(1, levels + 1)
    def _(d):
        pending = [functools.partial(pass_on, d, k) for k in range(4)]
        pending.append(functools.partial(pass_across, d))

        def between():
            if pending:
                pending.pop(0)()

        between()
        between()
        work(d - 1, between)

    for k in (2, 3, 1):
        first(k).wait_send()
    copy(ACROSS, f, 0, packed.at[e]).wait_send()
    along(f, 0, sent, src=packed.at[e])
    for k in (1, 2, 3):
        along(f, k, sent)
        copy(ACROSS, f, k).wait_send()
    along(across, 0, sent)
    for d in range(1, levels):

        @pl.when(z >= d)
        def _():
            for k in (0, 1, 2, 3):
                along(f - 2 * d, k, sent, down=False)
                if k > 0:
                    copy(ACROSS, f - 2 * d, k).wait_send()
            along(across - 2 * d, 0, sent, down=False)

        @pl.when(z + d < levels)
        def _():
            for k in (0, 1, 2, 3):
                along(f + 2 * d, k, sent, up=False)
                if k > 0:
                    copy(ACROSS, f + 2 * d, k).wait_send()
            along(across + 2 * d, 0, sent, up=False)


def gather_rows(packed, gate_part, up_part, grad_part, members):
    owners, height, model = packed.shape
    groups, _, width = gate_part.shape
    dtype = packed.dtype
    spread = (groups, owners, members * CAP)
    narrow = jax.ShapeDtypeStruct(spread + (width,), dtype)
    pair = (groups, owners, 2 * CAP)
    return pl.pallas_call(
        functools.partial(gather_kernel, members // 2, min(256, width)),
        out_shape=(
            jax.ShapeDtypeStruct((members, owners, height, model), dtype),
            jax.ShapeDtypeStruct(spread + (model,), dtype),
            narrow,
            narrow,
            narrow,
        ),
        in_specs=[pl.BlockSpec(memory_space=pl.ANY)] * 4,
        out_specs=(pl.BlockSpec(memory_space=pl.ANY),) * 5,
        scratch_shapes=[
            pltpu.VMEM((groups, model, width), dtype),
            pltpu.VMEM((groups, model, width), dtype),
            pltpu.VMEM((2, owners, height, model), dtype),
            pltpu.VMEM(pair + (width,), dtype),
            pltpu.VMEM(pair + (model,), dtype),
            pltpu.VMEM(pair + (width,), dtype),
            pltpu.VMEM(pair + (width,), dtype),
            pltpu.VMEM(pair + (width,), dtype),
            pltpu.SemaphoreType.DMA((3, members, owners)),
            pltpu.SemaphoreType.DMA((owners,)),
            pltpu.SemaphoreType.DMA((members, owners)),
            pltpu.SemaphoreType.DMA,
            pltpu.SemaphoreType.DMA((4,)),
            pltpu.SemaphoreType.DMA((4,)),
        ],
        compiler_params=pltpu.CompilerParams(
            collective_id=0, has_side_effects=True, vmem_limit_bytes=60 * 1024 * 1024
        ),
    )(packed, gate_part, up_part, grad_part.reshape(spread + (width,)))


def grad_kernel(rows_ref, gate_ref, up_ref, hidden_ref, hidden_out, gate_out, up_out):
    turned = rows_ref[...].T
    gate_out[...] = jnp.dot(turned, gate_ref[...], preferred_element_type=jnp.float32)
    up_out[...] = jnp.dot(turned, up_ref[...], preferred_element_type=jnp.float32)
    hidden_out[...] = hidden_ref[...]


def weight_grads(rows, gate_delta, up_delta, hidden):
    groups, slots, model = rows.shape
    width = gate_delta.shape[2]
    tile = min(512, model)
    steps = model // tile
    delta = pl.BlockSpec((None, slots, width), lambda g, m: (g, 0, 0))
    part = pl.BlockSpec((None, slots // steps, width), lambda g, m: (g, m, 0))
    out = pl.BlockSpec((None, tile, width), lambda g, m: (g, m, 0))
    shape = jax.ShapeDtypeStruct((groups, model, width), jnp.float32)
    return pl.pallas_call(
        grad_kernel,
        grid=(groups, steps),
        out_shape=(jax.ShapeDtypeStruct(hidden.shape, hidden.dtype), shape, shape),
        in_specs=[
            pl.BlockSpec((None, slots, tile), lambda g, m: (g, 0, m)),
            delta,
            delta,
            part,
        ],
        out_specs=(part, out, out),
        compiler_params=pltpu.CompilerParams(vmem_limit_bytes=60 * 1024 * 1024),
        cost_estimate=pl.CostEstimate(
            flops=4 * groups * slots * model * width,
            bytes_accessed=2 * groups * slots * (model + 4 * width) + 8 * groups * model * width,
            transcendentals=0,
        ),
    )(rows, gate_delta, up_delta, hidden)


def pack_kernel(ids_ref, tokens_ref, packed_ref):
    count = tokens_ref.shape[0]
    slots = packed_ref.shape[0]
    ids = ids_ref[...]
    lanes = lax.broadcasted_iota(jnp.int32, (count, 128), 1)
    onehot = jnp.where(ids == lanes, 1.0, 0.0)
    earlier = lax.broadcasted_iota(jnp.int32, (count, count), 1)
    later = lax.broadcasted_iota(jnp.int32, (count, count), 0)
    lower = jnp.where(earlier < later, 1.0, 0.0).astype(jnp.bfloat16)
    before = jnp.dot(lower, onehot.astype(jnp.bfloat16), preferred_element_type=jnp.float32)
    rank = jnp.sum(before * onehot, axis=1, keepdims=True)
    target = ids * CAP + rank.astype(jnp.int32)
    places = lax.broadcasted_iota(jnp.int32, (count, slots), 1)
    placing = jnp.where(places == target, 1.0, 0.0).T.astype(jnp.bfloat16)
    packed = jnp.dot(placing, tokens_ref[...], preferred_element_type=jnp.float32)
    packed_ref[...] = packed.astype(packed_ref.dtype)


def pack(expert_ids, tokens, experts):
    return pl.pallas_call(
        pack_kernel,
        out_shape=jax.ShapeDtypeStruct((experts * CAP, tokens.shape[1]), tokens.dtype),
        compiler_params=pltpu.CompilerParams(vmem_limit_bytes=32 * 1024 * 1024),
    )(expert_ids, tokens)


def on_device(tokens, expert_ids, gate_weight, up_weight, hidden_grad):
    owners = lax.axis_size("expert")
    members = lax.axis_size("fsdp")
    per_owner, model = gate_weight.shape[:2]
    packed = pack(expert_ids, tokens, per_owner * owners)
    blocks = packed.reshape(owners, per_owner * CAP, model)
    _, rows, hidden, gate_delta, up_delta = gather_rows(
        blocks, gate_weight, up_weight, hidden_grad, members
    )

    def by_slot(x):
        return x.reshape(per_owner, owners * members * CAP, x.shape[3])

    return weight_grads(by_slot(rows), by_slot(gate_delta), by_slot(up_delta), by_slot(hidden))


def solution(mesh):
    in_specs = (
        P(("expert", "fsdp"), None),
        P(("expert", "fsdp"), None),
        P("expert", None, "fsdp"),
        P("expert", None, "fsdp"),
        P("expert", None, "fsdp"),
    )
    out_specs = (P("expert", None, "fsdp"), P("expert", None, "fsdp"), P("expert", None, "fsdp"))
    return jax.shard_map(
        on_device, mesh=mesh, in_specs=in_specs, out_specs=out_specs, check_vma=False
    )
```
